1024 devices in a mesh: orb: 32 (over x, y_hi), bas: 32 (over y_lo, z, core).
Axes of the slice: x: 8, y: 8 (y_hi: 4, y_lo: 2; y = y_hi * 2 + y_lo), z: 8, core: 2. Of those that a mesh axis runs over, the one named last changes fastest.
Arguments:
- three_centre: bfloat16 [64, 32768, 256], P('bas', 'orb'), may hold values from -0.375 to 0.375
- occ_coeff: bfloat16 [512, 1024], P('orb'), may hold values from -1.5 to 1.5
- amp_coeff: bfloat16 [512, 1024], P('orb'), may hold values from -1.5 to 1.5
- col_blocks: int32 [32, 2], P('orb'), may hold values from 0 to 7, as said below
- slot_map: int32 [32, 64], P('orb'), may hold values from 0 to 63, as said below
- pair_list: int32 [32, 32, 32], P('orb', 'bas'), may hold values from 0 to 63, as said below
- pair_count: int32 [32, 32], P('orb', 'bas'), may hold values from 1 to 32, as said below
Outputs:
- exchange_blocks: float32 [32, 64, 128, 128], P('orb', 'bas')
The draws below stay inside these ranges and needn't reach their ends.
Inputs may be any that keep to these rules, and one draw needn't show every extreme that they name: `col_blocks`: each row group names 2 different column blocks. Each row of slot_map takes every value once; slot t is held by index t // 2 of bas. `pair_list`: the first pair_count entries of a list are different block pairs, the rest are unused; of the pairs whose slots one index of bas holds, a list names at most 1 among its used entries, and in every draw some index of bas is named 1 times by every list of a row group. `pair_count`: in every row group some slab's list uses all 32 entries.
All inputs are finite; a program needn't handle non-finite values.
Results may differ from the reference program's by a relative error of at most 0.02.
Values may be sent and summed in bfloat16 or wider, within the bound.
No kernel may reach another device: no remote copies, remote signals or barrier semaphores. Data moves between devices by JAX's collectives and lax.ppermute only.
A program may use at most 32 MiB of HBM per device.

```python
import jax
import jax.numpy as jnp
from jax import lax

BLK = 128
RB = 8
NCB = 2
NLB = 8
AUX_DEV = 2
NAUX = 64
ROWS = 32768
OCC = 512
NBF = 1024
NKB = 64
OWN = 2
CAP = 1
PMAX = 32
N_ORB = 32
N_BAS = 32


def owner_layout(key):
    base = jax.random.fold_in(key, 101)
    scores = jax.random.randint(base, (N_ORB, NKB), 0, 2 ** 20) * NKB + jnp.arange(NKB)[None, :]
    return jnp.argsort(scores, axis=1).astype(jnp.int32)


def task_layout(key):
    layout = owner_layout(key)
    base = jax.random.fold_in(key, 202)
    keys = jax.random.split(base, 5)
    level = jax.random.randint(keys[0], (N_ORB, N_BAS, 1, 1), 1, 8)
    full_slab = jax.random.randint(keys[4], (N_ORB, 1, 1, 1), 0, N_BAS)
    slab_ids = jnp.arange(N_BAS).reshape(1, N_BAS, 1, 1)
    level = jnp.where(slab_ids == full_slab, 8, level)
    trial = jax.random.randint(keys[1], (N_ORB, N_BAS, N_BAS, CAP), 0, 8)
    forced = jax.random.randint(keys[2], (N_ORB, 1, 1, 1), 0, N_BAS)
    owners = jnp.arange(N_BAS).reshape(1, 1, N_BAS, 1)
    picked = (trial < level) | (owners == forced)
    scores = jax.random.randint(keys[3], (N_ORB, N_BAS, N_BAS, OWN), 0, 2 ** 20) * OWN + jnp.arange(OWN)
    local_slots = jnp.argsort(scores, axis=3)[..., :CAP]
    slots = owners * OWN + local_slots
    flat_slots = slots.reshape(N_ORB, N_BAS, PMAX)
    flat_picked = picked.reshape(N_ORB, N_BAS, PMAX).astype(jnp.int32)
    ordering = jnp.argsort(1 - flat_picked, axis=2, stable=True)
    sorted_slots = jnp.take_along_axis(flat_slots, ordering, axis=2)
    inverse = jnp.argsort(layout, axis=1)
    inverse = jnp.broadcast_to(inverse[:, None, :], (N_ORB, N_BAS, NKB))
    pairs = jnp.take_along_axis(inverse, sorted_slots, axis=2)
    counts = jnp.sum(flat_picked, axis=2)
    return (pairs.astype(jnp.int32), counts.astype(jnp.int32))


def draw_col_blocks(key, part):
    key = jax.random.fold_in(key, 5)
    scores = jax.random.randint(key, (N_ORB, NLB), 0, 2 ** 20) * NLB + jnp.arange(NLB)[None, :]
    return jnp.argsort(scores, axis=1)[:, :NCB].astype(jnp.int32)


def draw_slot_map(key, part):
    layout = owner_layout(key)
    return layout


def draw_pair_list(key, part):
    pairs, counts = task_layout(key)
    return pairs


def draw_pair_count(key, part):
    pairs, counts = task_layout(key)
    return counts


def level_of(rng, shape, cuts, smallest, high):
    def one(axis_at, blocks):
        steps = jax.random.uniform(jax.random.fold_in(jax.random.fold_in(rng, 6), axis_at), (blocks,), jnp.float32, smallest / len(cuts), high / len(cuts))
        return jnp.repeat(jnp.exp(steps), shape[axis_at] // blocks).reshape((-1,) + (1,) * (len(shape) - axis_at - 1))

    factor_of = one(*cuts[0])
    for cut in cuts[1:]:
        factor_of = factor_of * one(*cut)
    return factor_of


def noise(rng, extent, deviation, bound, cuts=(), kind=jnp.bfloat16):
    drawn = deviation * jax.random.normal(rng, extent, jnp.float32)
    if cuts:
        drawn = drawn * level_of(rng, extent, cuts, -0.22, 0.18)
    return jnp.clip(drawn, -bound, bound).astype(kind)


def setup_inputs(seed: int = 0) -> dict:
    streams_of = jax.random.split(jax.random.key(seed), 8)
    three_centre = noise(streams_of[0], (NAUX, ROWS, NCB * BLK), (NCB * BLK) ** -0.5, 0.375, ((0, 32), (1, 32)))
    occ_coeff = noise(streams_of[1], (OCC, NBF), ((OCC * AUX_DEV * N_BAS // 4) ** -0.25), 1.5, ((0, 32),))
    amp_coeff = noise(streams_of[2], (OCC, NBF), ((OCC * AUX_DEV * N_BAS // 4) ** -0.25), 1.5, ((0, 32),))
    col_blocks = draw_col_blocks(jax.random.fold_in(streams_of[7], 71), 0)
    slot_map = draw_slot_map(jax.random.fold_in(streams_of[7], 71), 0)
    pair_list = draw_pair_list(jax.random.fold_in(streams_of[7], 71), 0)
    pair_count = draw_pair_count(jax.random.fold_in(streams_of[7], 71), 0)
    return dict(three_centre=three_centre, occ_coeff=occ_coeff, amp_coeff=amp_coeff, col_blocks=col_blocks, slot_map=slot_map, pair_list=pair_list, pair_count=pair_count)


def reference(three_centre, occ_coeff, amp_coeff, col_blocks, slot_map, pair_list, pair_count):
    rows_dev = RB * BLK
    width = NCB * BLK
    integrals = three_centre.reshape(N_BAS, AUX_DEV, N_ORB, rows_dev, width)

    def per_group(group):
        columns = col_blocks[group]
        occ_sel = jnp.concatenate([lax.dynamic_slice_in_dim(occ_coeff, columns[k] * BLK, BLK, 1) for k in range(NCB)], 1)
        amp_sel = jnp.concatenate([lax.dynamic_slice_in_dim(amp_coeff, columns[k] * BLK, BLK, 1) for k in range(NCB)], 1)

        def per_slab(total, slab_index):
            slab = integrals[slab_index, :, group].reshape(AUX_DEV * rows_dev, width)
            occ_half = jnp.dot(occ_sel, slab.T, preferred_element_type=jnp.float32).astype(jnp.bfloat16)
            amp_half = jnp.dot(amp_sel, slab.T, preferred_element_type=jnp.float32).astype(jnp.bfloat16)
            product = jnp.dot(occ_half.reshape(OCC * AUX_DEV, rows_dev).T, amp_half.reshape(OCC * AUX_DEV, rows_dev), preferred_element_type=jnp.float32)
            blocks = product.reshape(RB, BLK, RB, BLK).transpose(0, 2, 1, 3).reshape(NKB, BLK, BLK)
            valid = (jnp.arange(PMAX, dtype=jnp.int32) < pair_count[group, slab_index]).astype(jnp.float32)
            listed = jnp.zeros((NKB,), jnp.float32).at[pair_list[group, slab_index]].max(valid)
            rounded = (blocks * listed[:, None, None]).astype(jnp.bfloat16)
            rounded = lax.optimization_barrier(rounded)
            return total + rounded.astype(jnp.float32), None

        total, _ = lax.scan(per_slab, jnp.zeros((NKB, BLK, BLK), jnp.float32), jnp.arange(N_BAS, dtype=jnp.int32))
        return jnp.zeros((NKB, BLK, BLK), jnp.float32).at[slot_map[group]].set(total)

    return lax.map(per_group, jnp.arange(N_ORB, dtype=jnp.int32))
```

```python
import jax
import jax.numpy as jnp
from jax import lax
from jax.experimental import pallas as pl
from jax.experimental.pallas import tpu as pltpu
from jax.sharding import Mesh, PartitionSpec as P

BLK = 128
NCB = 2
ORB = ("x", "yh")
BAS = ("yl", "z", "c")
TAG = 8
F32 = jnp.float32
BF16 = jnp.bfloat16


def contract(a, b, da, db):
    return lax.dot_general(a, b, (((da,), (db,)), ((), ())), preferred_element_type=F32)


def exchange_kernel(pairs, count, slots, own, other, g_ref, out, blocks, place, tag):
    owners = out.shape[0]
    aux, rows, _ = g_ref.shape
    row_blocks = rows // BLK

    def clear(d, _):
        place[d] = 0
        tag[d] = 2
        return 0

    lax.fori_loop(0, owners, clear, 0, unroll=True)

    def enter(e, _):
        p = pairs[0, 0, e]
        slot = slots[0, p]
        d = slot // 2
        place[d] = p
        tag[d] = slot - 2 * d
        return 0

    lax.fori_loop(0, count[0, 0], enter, 0)

    def wide(ref, t):
        return jnp.concatenate([ref[t, k] for k in range(NCB)], axis=1)

    s = contract(wide(own, 0), wide(own, 1), 0, 0) + contract(wide(other, 0), wide(other, 1), 0, 0)
    s = s.astype(BF16)
    g = jnp.concatenate([g_ref[q] for q in range(aux)], axis=1)
    step = 2 * BLK
    for m in range(rows // step):
        t = jnp.concatenate(
            [contract(g_ref[q, m * step:(m + 1) * step], s, 1, 0).astype(BF16) for q in range(aux)], axis=1
        )
        full = contract(t, g, 1, 1).astype(BF16)
        for h in range(2):
            for n in range(row_blocks):
                blocks[(2 * m + h) * row_blocks + n] = full[h * BLK:(h + 1) * BLK, n * BLK:(n + 1) * BLK]

    def send(d, _):
        out[d, 0:BLK] = blocks[place[d]]
        out[d, BLK:BLK + TAG] = jnp.full((TAG, BLK), tag[d], jnp.int32).astype(F32).astype(BF16)
        return 0

    lax.fori_loop(0, owners, send, 0, unroll=4)


def sum_kernel(got, out):
    def add(d, total):
        mark = got[d, BLK:BLK + TAG].astype(F32)
        piece = got[d, 0:BLK].astype(F32).reshape(BLK // TAG, TAG, BLK)
        return tuple(
            total[k] + jnp.where((mark == k)[None], piece, 0.0) for k in range(2)
        )

    zero = jnp.zeros((BLK // TAG, TAG, BLK), F32)
    total = lax.fori_loop(0, got.shape[0], add, (zero, zero))
    for k in range(2):
        out[0, k] = total[k].reshape(BLK, BLK)


def on_device(three_centre, occ_coeff, amp_coeff, col_blocks, slot_map, pair_list, pair_count):
    n_orb = lax.axis_size(ORB)
    n_bas = lax.axis_size(BAS)
    own_rows, width = occ_coeff.shape
    half = own_rows // 2
    col_total = width // BLK
    core = lax.axis_index("c")

    def cut(coeff):
        part = lax.dynamic_slice_in_dim(coeff, core * half, half, 0)
        return part.reshape(half, col_total, BLK).transpose(1, 0, 2)

    mine = jnp.concatenate([cut(occ_coeff), cut(amp_coeff)], 0)
    mine = jnp.broadcast_to(mine.reshape(1, 2 * col_total * half, BLK), (n_orb, 2 * col_total * half, BLK))
    got = lax.all_to_all(mine, ORB, 0, 0, tiled=True)
    got = got.reshape(n_orb, 2, col_total, half, BLK)
    own = jnp.stack(
        [lax.dynamic_index_in_dim(got, col_blocks[0, k], 2, keepdims=False) for k in range(NCB)], 0
    )
    own = own.transpose(2, 0, 1, 3, 4).reshape(2, NCB, n_orb * half, BLK)
    other = lax.ppermute(own, "c", [(0, 1), (1, 0)])

    vmem = pl.BlockSpec(memory_space=pltpu.VMEM)
    smem = pl.BlockSpec(memory_space=pltpu.SMEM)
    row_blocks = three_centre.shape[1] // BLK
    send = pl.pallas_call(
        exchange_kernel,
        out_shape=jax.ShapeDtypeStruct((n_bas, BLK + TAG, BLK), BF16),
        in_specs=[smem, smem, smem, vmem, vmem, vmem],
        out_specs=vmem,
        scratch_shapes=[
            pltpu.VMEM((row_blocks * row_blocks, BLK, BLK), BF16),
            pltpu.SMEM((n_bas,), jnp.int32),
            pltpu.SMEM((n_bas,), jnp.int32),
        ],
        compiler_params=pltpu.CompilerParams(vmem_limit_bytes=40 * 1024 * 1024),
        name="exchange_blocks",
    )(pair_list, pair_count, slot_map, own, other, three_centre)
    arrived = lax.all_to_all(send, BAS, 0, 0, tiled=True)
    return pl.pallas_call(
        sum_kernel,
        out_shape=jax.ShapeDtypeStruct((1, 2, BLK, BLK), F32),
        in_specs=[vmem],
        out_specs=vmem,
        compiler_params=pltpu.CompilerParams(vmem_limit_bytes=40 * 1024 * 1024),
        name="sum_slots",
    )(arrived)


def solution(mesh):
    fine = Mesh(mesh.devices.reshape(8, 4, 2, 8, 2), ("x", "yh", "yl", "z", "c"))
    placed = (
        P(BAS, ORB, None),
        P(ORB, None),
        P(ORB, None),
        P(ORB, None),
        P(ORB, None),
        P(ORB, BAS, None),
        P(ORB, BAS),
    )
    return jax.shard_map(
        on_device,
        mesh=fine,
        in_specs=placed,
        out_specs=P(ORB, BAS, None, None),
        check_vma=False,
    )
```

```python
import jax
import jax.numpy as jnp
from jax import lax
from jax.experimental import pallas as pl
from jax.experimental.pallas import tpu as pltpu
from jax.sharding import Mesh, PartitionSpec as P

BLK = 128
NCB = 2
ORB = ("x", "yh")
BAS = ("yl", "z", "c")
TAG = 8
F32 = jnp.float32
BF16 = jnp.bfloat16


def contract(a, b, da, db):
    return lax.dot_general(a, b, (((da,), (db,)), ((), ())), preferred_element_type=F32)


def exchange_kernel(pairs, count, slots, near, far, g_ref, out, blocks, place, tag):
    owners = out.shape[0]
    aux, rows, _ = g_ref.shape
    row_blocks = rows // BLK

    def clear(d, _):
        place[d] = 0
        tag[d] = 2
        return 0

    lax.fori_loop(0, owners, clear, 0, unroll=True)

    def enter(e, _):
        p = pairs[0, 0, e]
        slot = slots[0, p]
        d = slot // 2
        place[d] = p
        tag[d] = slot - 2 * d
        return 0

    lax.fori_loop(0, count[0, 0], enter, 0)

    def wide(t):
        return jnp.concatenate(
            [jnp.concatenate([ref[t, k] for k in range(NCB)], axis=1) for ref in (near, far)], axis=0
        )

    first, second = wide(0), wide(1)
    is_occ = lax.axis_index("yl") == 0
    s = contract(jnp.where(is_occ, first, second), jnp.where(is_occ, second, first), 0, 0)
    s = s.astype(BF16)
    g = jnp.concatenate([g_ref[q] for q in range(aux)], axis=1)
    step = 2 * BLK
    for m in range(rows // step):
        t = jnp.concatenate(
            [contract(g_ref[q, m * step:(m + 1) * step], s, 1, 0).astype(BF16) for q in range(aux)], axis=1
        )
        full = contract(t, g, 1, 1).astype(BF16)
        for h in range(2):
            for n in range(row_blocks):
                blocks[(2 * m + h) * row_blocks + n] = full[h * BLK:(h + 1) * BLK, n * BLK:(n + 1) * BLK]

    def send(d, _):
        out[d, 0:BLK] = blocks[place[d]]
        out[d, BLK:BLK + TAG] = jnp.full((TAG, BLK), tag[d], jnp.int32).astype(F32).astype(BF16)
        return 0

    lax.fori_loop(0, owners, send, 0, unroll=4)


def sum_kernel(got, out):
    def add(d, total):
        mark = got[d, BLK:BLK + TAG].astype(F32)
        piece = got[d, 0:BLK].astype(F32).reshape(BLK // TAG, TAG, BLK)
        return tuple(
            total[k] + jnp.where((mark == k)[None], piece, 0.0) for k in range(2)
        )

    zero = jnp.zeros((BLK // TAG, TAG, BLK), F32)
    total = lax.fori_loop(0, got.shape[0], add, (zero, zero))
    for k in range(2):
        out[0, k] = total[k].reshape(BLK, BLK)


def on_device(three_centre, occ_coeff, amp_coeff, col_blocks, slot_map, pair_list, pair_count):
    n_orb = lax.axis_size(ORB)
    n_bas = lax.axis_size(BAS)
    own_rows, width = occ_coeff.shape
    half = own_rows // 2
    col_total = width // BLK
    swap = [(0, 1), (1, 0)]

    tensor = jnp.where(lax.axis_index("yl") == 0, occ_coeff, amp_coeff)
    mine = lax.dynamic_slice_in_dim(tensor, lax.axis_index("c") * half, half, 0)
    mine = mine.reshape(half, col_total, BLK).transpose(1, 0, 2).reshape(1, col_total * half, BLK)
    mine = jnp.broadcast_to(mine, (n_orb, col_total * half, BLK))
    got = lax.all_to_all(mine, ORB, 0, 0, tiled=True).reshape(n_orb, col_total, half, BLK)
    own = jnp.stack(
        [
            lax.dynamic_index_in_dim(got, col_blocks[0, k], 1, keepdims=False).reshape(n_orb * half, BLK)
            for k in range(NCB)
        ],
        0,
    )
    other = lax.ppermute(own, "yl", swap)
    near = jnp.stack((own, other), 0)
    far = lax.ppermute(near, "c", swap)
    coeffs = (near, far)

    vmem = pl.BlockSpec(memory_space=pltpu.VMEM)
    smem = pl.BlockSpec(memory_space=pltpu.SMEM)
    row_blocks = three_centre.shape[1] // BLK
    send = pl.pallas_call(
        exchange_kernel,
        out_shape=jax.ShapeDtypeStruct((n_bas, BLK + TAG, BLK), BF16),
        in_specs=[smem, smem, smem] + [vmem] * (len(coeffs) + 1),
        out_specs=vmem,
        scratch_shapes=[
            pltpu.VMEM((row_blocks * row_blocks, BLK, BLK), BF16),
            pltpu.SMEM((n_bas,), jnp.int32),
            pltpu.SMEM((n_bas,), jnp.int32),
        ],
        compiler_params=pltpu.CompilerParams(vmem_limit_bytes=40 * 1024 * 1024),
        name="exchange_blocks",
    )(pair_list, pair_count, slot_map, *coeffs, three_centre)
    arrived = lax.all_to_all(send, BAS, 0, 0, tiled=True)
    return pl.pallas_call(
        sum_kernel,
        out_shape=jax.ShapeDtypeStruct((1, 2, BLK, BLK), F32),
        in_specs=[vmem],
        out_specs=vmem,
        compiler_params=pltpu.CompilerParams(vmem_limit_bytes=40 * 1024 * 1024),
        name="sum_slots",
    )(arrived)


def solution(mesh):
    fine = Mesh(mesh.devices.reshape(8, 4, 2, 8, 2), ("x", "yh", "yl", "z", "c"))
    placed = (
        P(BAS, ORB, None),
        P(ORB, None),
        P(ORB, None),
        P(ORB, None),
        P(ORB, None),
        P(ORB, BAS, None),
        P(ORB, BAS),
    )
    return jax.shard_map(
        on_device,
        mesh=fine,
        in_specs=placed,
        out_specs=P(ORB, BAS, None, None),
        check_vma=False,
    )
```

```python
import jax
import jax.numpy as jnp
from jax import lax
from jax.experimental import pallas as pl
from jax.experimental.pallas import tpu as pltpu
from jax.sharding import Mesh, PartitionSpec as P

BLK = 128
NCB = 2
OWN = 2
ORB = ("x", "yh")
FAR = ("yl", "zh")
BAS = ("yl", "zh", "zl", "c")
SWAP = ((0, 1), (1, 0))
F32 = jnp.float32
BF16 = jnp.bfloat16


def contract(a, b, da, db):
    return lax.dot_general(a, b, (((da,), (db,)), ((), ())), preferred_element_type=F32)


def exchange_kernel(*refs):
    listed, near, far, slabs, out, t_ref = refs[0:2], refs[2], refs[3], refs[4:8], refs[8], refs[9]
    owners = out.shape[0]
    aux, row_blocks, _, width = slabs[0].shape

    def wide(t):
        return jnp.concatenate(
            [jnp.concatenate([ref[t, k] for k in range(NCB)], axis=1) for ref in (near, far)], axis=0
        )

    first, second = wide(0), wide(1)
    is_occ = lax.axis_index("yl") == 0
    s = contract(jnp.where(is_occ, first, second), jnp.where(is_occ, second, first), 0, 0)
    s = s.astype(BF16)
    for k, g_ref in enumerate(slabs):
        for q in range(aux):
            for m in range(0, row_blocks, 2):
                t = contract(g_ref[q, m:m + 2].reshape(2 * BLK, width), s, 1, 0).astype(BF16)
                t_ref[k, q, m:m + 2] = t.reshape(2, BLK, width)

    quarter = lax.axis_index("zl") * 2 + lax.axis_index("c")

    def owner(j, _):
        slot = (j * 4 + quarter) * OWN
        total = [jnp.zeros((BLK, BLK), F32)] * OWN
        for k, g_ref in enumerate(slabs):
            pair = [listed[k // 2][k % 2, slot + h] for h in range(OWN)]
            p = jnp.maximum(jnp.maximum(pair[0], pair[1]), 0)
            row, col = p // row_blocks, p % row_blocks
            block = contract(t_ref[k, 0, row], g_ref[0, col], 1, 1)
            for q in range(1, aux):
                block = block + contract(t_ref[k, q, row], g_ref[q, col], 1, 1)
            total = [total[h] + jnp.where(pair[h] >= 0, block, 0.0) for h in range(OWN)]
        for h in range(OWN):
            out[j, h * BLK:(h + 1) * BLK] = total[h].astype(BF16)
        return 0

    lax.fori_loop(0, owners, owner, 0, unroll=2)


def select_kernel(columns, got, out):
    for k in range(NCB):
        out[k] = got[:, columns[0, k]]


def sum_kernel(got, out):
    for h in range(OWN):
        total = got[0, h * BLK:(h + 1) * BLK].astype(F32)
        for j in range(1, got.shape[0]):
            total = total + got[j, h * BLK:(h + 1) * BLK].astype(F32)
        out[0, h] = total


def listed_pairs(slot_map, pair_list, pair_count):
    slot = slot_map[0]
    ids = jnp.arange(slot.shape[0], dtype=jnp.int32)
    entry = pair_list[0, 0]
    used = jnp.arange(entry.shape[0], dtype=jnp.int32) < pair_count[0, 0]
    named = jnp.max(jnp.where(used[:, None] & (entry[:, None] == ids[None]), 1, 0), 0)
    at = (slot[:, None] == ids[None]) & (named[:, None] > 0)
    return jnp.max(jnp.where(at, ids[:, None], -1), 0)[None]


def on_device(three_centre, occ_coeff, amp_coeff, col_blocks, slot_map, pair_list, pair_count):
    n_orb = lax.axis_size(ORB)
    n_far = lax.axis_size(FAR)
    own_rows, width = occ_coeff.shape
    half = own_rows // 2
    col_total = width // BLK

    tensor = jnp.where(lax.axis_index("yl") == 0, occ_coeff, amp_coeff)
    mine = lax.dynamic_slice_in_dim(tensor, lax.axis_index("c") * half, half, 0)
    mine = mine.reshape(half, col_total, BLK).transpose(1, 0, 2).reshape(1, col_total * half, BLK)
    mine = jnp.broadcast_to(mine, (n_orb, col_total * half, BLK))
    got = lax.all_to_all(mine, ORB, 0, 0, tiled=True).reshape(n_orb, col_total, half, BLK)

    aux, rows, sel = three_centre.shape
    g = three_centre.reshape(aux, rows // BLK, BLK, sel)
    g_side = lax.ppermute(g, "zl", SWAP)
    g_core = lax.ppermute(g, "c", SWAP)
    listed = listed_pairs(slot_map, pair_list, pair_count)
    listed = jnp.concatenate((listed, lax.ppermute(listed, "zl", SWAP)), 0)
    listed_core = lax.ppermute(listed, "c", SWAP)
    got, listed_core = lax.optimization_barrier((got, listed_core))

    vmem = pl.BlockSpec(memory_space=pltpu.VMEM)
    smem = pl.BlockSpec(memory_space=pltpu.SMEM)
    own = pl.pallas_call(
        select_kernel,
        out_shape=jax.ShapeDtypeStruct((NCB, n_orb, half, BLK), BF16),
        in_specs=[smem, vmem],
        out_specs=vmem,
        name="select_columns",
    )(col_blocks, got).reshape(NCB, n_orb * half, BLK)
    g_side, own = lax.optimization_barrier((g_side, own))
    g_both = lax.ppermute(g_side, "c", SWAP)
    near = jnp.stack((own, lax.ppermute(own, "yl", SWAP)), 0)
    far = lax.ppermute(near, "c", SWAP)
    slabs = (g, g_side, g_core, g_both)

    send = pl.pallas_call(
        exchange_kernel,
        out_shape=jax.ShapeDtypeStruct((n_far, OWN * BLK, BLK), BF16),
        in_specs=[smem] * 2 + [vmem] * (2 + len(slabs)),
        out_specs=vmem,
        scratch_shapes=[pltpu.VMEM((len(slabs), aux, rows // BLK, BLK, sel), BF16)],
        compiler_params=pltpu.CompilerParams(vmem_limit_bytes=40 * 1024 * 1024),
        name="exchange_blocks",
    )(listed, listed_core, near, far, *slabs)
    arrived = lax.all_to_all(send, FAR, 0, 0, tiled=True)
    return pl.pallas_call(
        sum_kernel,
        out_shape=jax.ShapeDtypeStruct((1, OWN, BLK, BLK), F32),
        in_specs=[vmem],
        out_specs=vmem,
        compiler_params=pltpu.CompilerParams(vmem_limit_bytes=40 * 1024 * 1024),
        name="sum_slots",
    )(arrived)


def solution(mesh):
    fine = Mesh(mesh.devices.reshape(8, 4, 2, 4, 2, 2), ("x", "yh", "yl", "zh", "zl", "c"))
    placed = (
        P(BAS, ORB, None),
        P(ORB, None),
        P(ORB, None),
        P(ORB, None),
        P(ORB, None),
        P(ORB, BAS, None),
        P(ORB, BAS),
    )
    return jax.shard_map(
        on_device,
        mesh=fine,
        in_specs=placed,
        out_specs=P(ORB, BAS, None, None),
        check_vma=False,
    )
```

```python
import jax
import jax.numpy as jnp
from jax import lax
from jax.experimental import pallas as pl
from jax.experimental.pallas import tpu as pltpu
from jax.sharding import Mesh, PartitionSpec as P

BLK = 128
NCB = 2
OWN = 2
AUX = 2
TILE = 16
ORB = ("x", "yh")
FAR = ("yl", "zh")
BAS = ("yl", "zh", "zl", "c")
SWAP = ((0, 1), (1, 0))
F32 = jnp.float32
BF16 = jnp.bfloat16


def contract(a, b, da, db):
    return lax.dot_general(a, b, (((da,), (db,)), ((), ())), preferred_element_type=F32)


def prepare_kernel(pairs, count, slots, occ, amp, g_ref, mine, packed):
    half = occ.shape[0] // 2
    tensor = jnp.where(lax.axis_index("yl") == 0, occ[...].astype(F32), amp[...].astype(F32))
    tensor = jnp.where(lax.axis_index("c") == 0, tensor[:half], tensor[half:])
    parts = [tensor[:, n * BLK:(n + 1) * BLK] for n in range(tensor.shape[1] // BLK)]
    block = jnp.concatenate(parts, axis=0).astype(BF16)
    for i in range(mine.shape[0]):
        mine[i] = block

    rows, width = g_ref.shape
    packed[0:rows] = g_ref[...]
    lane = lax.broadcasted_iota(jnp.int32, (TILE, width), 1)
    listed = jnp.full((TILE, width), -1, jnp.int32)
    for e in range(pairs.shape[2]):
        p = pairs[0, 0, e]
        here = jnp.where(e < count[0, 0], slots[0, p], -1)
        listed = jnp.where(lane == here, p, listed)
    packed[rows:rows + TILE] = listed.astype(F32).astype(BF16)


def exchange_kernel(*refs):
    near, far, slabs = refs[0], refs[1], refs[2:6]
    out, t_ref, held, wide_list, listed, sem, held_sem = refs[6:]
    fetches = [pltpu.make_async_copy(slabs[2 + i], held.at[i], held_sem.at[i]) for i in range(2)]
    for fetch in fetches:
        fetch.start()
    slabs = [slabs[0], slabs[1], held.at[0], held.at[1]]
    rows, width = t_ref.shape[1:]
    aux_blocks = rows // BLK
    row_blocks = aux_blocks // AUX

    def wide(t):
        return jnp.concatenate(
            [jnp.concatenate([ref[t, k] for k in range(NCB)], axis=1) for ref in (near, far)], axis=0
        )

    first, second = wide(0), wide(1)
    is_occ = lax.axis_index("yl") == 0
    s = contract(jnp.where(is_occ, first, second), jnp.where(is_occ, second, first), 0, 0)
    s = s.astype(BF16)
    step = 2 * BLK
    for k, g_ref in enumerate(slabs):
        if k >= 2:
            fetches[k - 2].wait()
        wide_list[k] = g_ref[rows:rows + TILE, 0:BLK].astype(F32).astype(jnp.int32)
        if k == 3:
            copy = pltpu.make_async_copy(wide_list, listed, sem)
            copy.start()
        for m in range(0, rows, step):
            t_ref[k, m:m + step] = contract(g_ref[m:m + step], s, 1, 0).astype(BF16)
    copy.wait()

    quarter = lax.axis_index("zl") * 2 + lax.axis_index("c")

    def owner(j, _):
        slot = (j * 4 + quarter) * OWN
        total = [jnp.zeros((BLK, BLK), F32)] * OWN
        for k, g_ref in enumerate(slabs):
            pair = [listed[k, 0, slot + h] for h in range(OWN)]
            p = jnp.maximum(jnp.maximum(pair[0], pair[1]), 0)
            block = None
            for q in range(AUX):
                at = [
                    pl.ds(pl.multiple_of((q * row_blocks + r) * BLK, BLK), BLK)
                    for r in (p // row_blocks, p % row_blocks)
                ]
                term = contract(t_ref[k, at[0]], g_ref[at[1]], 1, 1)
                block = term if block is None else block + term
            total = [total[h] + jnp.where(pair[h] >= 0, block, 0.0) for h in range(OWN)]
        for h in range(OWN):
            out[j, h * BLK:(h + 1) * BLK] = total[h].astype(BF16)
        return 0

    lax.fori_loop(0, out.shape[0], owner, 0, unroll=2)


def select_kernel(columns, got, *rest):
    out = rest[-1]
    for k in range(NCB):
        out[k] = got[:, columns[0, k]]


def sum_kernel(got, out):
    for h in range(OWN):
        total = got[0, h * BLK:(h + 1) * BLK].astype(F32)
        for j in range(1, got.shape[0]):
            total = total + got[j, h * BLK:(h + 1) * BLK].astype(F32)
        out[0, h] = total


def on_device(three_centre, occ_coeff, amp_coeff, col_blocks, slot_map, pair_list, pair_count):
    n_orb = lax.axis_size(ORB)
    n_far = lax.axis_size(FAR)
    own_rows, width = occ_coeff.shape
    half = own_rows // 2
    col_total = width // BLK

    aux, rows, sel = three_centre.shape
    vmem = pl.BlockSpec(memory_space=pltpu.VMEM)
    smem = pl.BlockSpec(memory_space=pltpu.SMEM)
    mine, g = pl.pallas_call(
        prepare_kernel,
        out_shape=(
            jax.ShapeDtypeStruct((n_orb, col_total * half, BLK), BF16),
            jax.ShapeDtypeStruct((aux * rows + TILE, sel), BF16),
        ),
        in_specs=[smem] * 3 + [vmem] * 3,
        out_specs=(vmem, vmem),
        name="prepare",
    )(pair_list, pair_count, slot_map, occ_coeff, amp_coeff, three_centre.reshape(aux * rows, sel))
    with jax.named_scope("g_side"):
        g_side = lax.ppermute(g, "zl", SWAP)
    with jax.named_scope("g_core"):
        g_core = lax.ppermute(g, "c", SWAP)
    with jax.named_scope("g_both"):
        g_both = lax.ppermute(g_side, "c", SWAP)
    got = lax.all_to_all(mine, ORB, 0, 0, tiled=True).reshape(n_orb, col_total, half, BLK)
    own = pl.pallas_call(
        select_kernel,
        out_shape=jax.ShapeDtypeStruct((NCB, n_orb, half, BLK), BF16),
        in_specs=[smem, vmem] + [pl.BlockSpec(memory_space=pl.ANY)] * 0,
        out_specs=vmem,
        compiler_params=pltpu.CompilerParams(vmem_limit_bytes=4 * 1024 * 1024),
        name="select_columns",
    )(col_blocks, got).reshape(NCB, n_orb * half, BLK)
    with jax.named_scope("other"):
        other = lax.ppermute(own, "yl", SWAP)
    near = jnp.stack((own, other), 0)
    with jax.named_scope("far"):
        far = lax.ppermute(near, "c", SWAP)
    coeffs = (near, far)
    slabs = (g, g_side, g_core, g_both)

    send = pl.pallas_call(
        exchange_kernel,
        out_shape=jax.ShapeDtypeStruct((n_far, OWN * BLK, BLK), BF16),
        in_specs=[vmem] * 4 + [pl.BlockSpec(memory_space=pl.ANY)] * 2,
        out_specs=vmem,
        scratch_shapes=[
            pltpu.VMEM((len(slabs), aux * rows, sel), BF16),
            pltpu.VMEM((2,) + g.shape, BF16),
            pltpu.VMEM((len(slabs), TILE, BLK), jnp.int32),
            pltpu.SMEM((len(slabs), TILE, BLK), jnp.int32),
            pltpu.SemaphoreType.DMA,
            pltpu.SemaphoreType.DMA((2,)),
        ],
        compiler_params=pltpu.CompilerParams(vmem_limit_bytes=12 * 1024 * 1024),
        name="exchange_blocks",
    )(*coeffs, *slabs)
    arrived = lax.all_to_all(send, FAR, 0, 0, tiled=True)
    return pl.pallas_call(
        sum_kernel,
        out_shape=jax.ShapeDtypeStruct((1, OWN, BLK, BLK), F32),
        in_specs=[vmem],
        out_specs=vmem,
        compiler_params=pltpu.CompilerParams(vmem_limit_bytes=12 * 1024 * 1024),
        name="sum_slots",
    )(arrived)


def solution(mesh):
    fine = Mesh(mesh.devices.reshape(8, 4, 2, 4, 2, 2), ("x", "yh", "yl", "zh", "zl", "c"))
    placed = (
        P(BAS, ORB, None),
        P(ORB, None),
        P(ORB, None),
        P(ORB, None),
        P(ORB, None),
        P(ORB, BAS, None),
        P(ORB, BAS),
    )
    return jax.shard_map(
        on_device,
        mesh=fine,
        in_specs=placed,
        out_specs=P(ORB, BAS, None, None),
        check_vma=False,
    )
```

```python
import jax
import jax.numpy as jnp
from jax import lax
from jax.experimental import pallas as pl
from jax.experimental.pallas import tpu as pltpu
from jax.sharding import Mesh, PartitionSpec as P

BLK = 128
NCB = 2
OWN = 2
AUX = 2
TILE = 16
ORB = ("x", "yh")
FAR = ("yl", "zh")
BAS = ("yl", "zh", "zl", "c")
SWAP = ((0, 1), (1, 0))
F32 = jnp.float32
BF16 = jnp.bfloat16


def contract(a, b, da, db):
    return lax.dot_general(a, b, (((da,), (db,)), ((), ())), preferred_element_type=F32)


def prepare_kernel(pairs, count, slots, occ, amp, g_ref, mine, packed):
    half = occ.shape[0] // 2
    tensor = jnp.where(lax.axis_index("yl") == 0, occ[...].astype(F32), amp[...].astype(F32))
    tensor = jnp.where(lax.axis_index("c") == 0, tensor[:half], tensor[half:])
    parts = [tensor[:, n * BLK:(n + 1) * BLK] for n in range(tensor.shape[1] // BLK)]
    block = jnp.concatenate(parts, axis=0).astype(BF16)
    for i in range(mine.shape[0]):
        mine[i] = block

    rows, width = g_ref.shape
    packed[0:rows] = g_ref[...]
    lane = lax.broadcasted_iota(jnp.int32, (TILE, width), 1)
    listed = jnp.full((TILE, width), -1, jnp.int32)
    for e in range(pairs.shape[2]):
        p = pairs[0, 0, e]
        here = jnp.where(e < count[0, 0], slots[0, p], -1)
        listed = jnp.where(lane == here, p, listed)
    packed[rows:rows + TILE] = listed.astype(F32).astype(BF16)


def exchange_kernel(*refs):
    near, far, slabs = refs[0], refs[1], refs[2:6]
    out, t_ref, held, wide_list, listed, sem, held_sem = refs[6:]
    fetches = [pltpu.make_async_copy(slabs[2 + i], held.at[i], held_sem.at[i]) for i in range(2)]
    for fetch in fetches:
        fetch.start()
    slabs = [slabs[0], slabs[1], held.at[0], held.at[1]]
    rows, width = t_ref.shape[1:]
    aux_blocks = rows // BLK
    row_blocks = aux_blocks // AUX

    def wide(t):
        return jnp.concatenate(
            [jnp.concatenate([ref[t, k] for k in range(NCB)], axis=1) for ref in (near, far)], axis=0
        )

    first, second = wide(0), wide(1)
    is_occ = lax.axis_index("yl") == 0
    s = contract(jnp.where(is_occ, first, second), jnp.where(is_occ, second, first), 0, 0)
    s = s.astype(BF16)
    step = 2 * BLK
    for k, g_ref in enumerate(slabs):
        if k >= 2:
            fetches[k - 2].wait()
        wide_list[k] = g_ref[rows:rows + TILE, 0:BLK].astype(F32).astype(jnp.int32)
        if k == 3:
            copy = pltpu.make_async_copy(wide_list, listed, sem)
            copy.start()
        for m in range(0, rows, step):
            t_ref[k, m:m + step] = contract(g_ref[m:m + step], s, 1, 0).astype(BF16)
    copy.wait()

    quarter = lax.axis_index("zl") * 2 + lax.axis_index("c")

    def owner(j, _):
        slot = (j * 4 + quarter) * OWN
        total = [jnp.zeros((BLK, BLK), F32)] * OWN
        for k, g_ref in enumerate(slabs):
            pair = [listed[k, 0, slot + h] for h in range(OWN)]
            p = jnp.maximum(jnp.maximum(pair[0], pair[1]), 0)
            block = None
            for q in range(AUX):
                at = [
                    pl.ds(pl.multiple_of((q * row_blocks + r) * BLK, BLK), BLK)
                    for r in (p // row_blocks, p % row_blocks)
                ]
                term = contract(t_ref[k, at[0]], g_ref[at[1]], 1, 1)
                block = term if block is None else block + term
            total = [total[h] + jnp.where(pair[h] >= 0, block, 0.0) for h in range(OWN)]
        for h in range(OWN):
            out[j, h * BLK:(h + 1) * BLK] = total[h].astype(BF16)
        return 0

    lax.fori_loop(0, out.shape[0], owner, 0, unroll=True)


def select_kernel(columns, got, *rest):
    out = rest[-1]
    for k in range(NCB):
        out[k] = got[:, columns[0, k]]


def sum_kernel(got, out):
    for h in range(OWN):
        total = got[0, h * BLK:(h + 1) * BLK].astype(F32)
        for j in range(1, got.shape[0]):
            total = total + got[j, h * BLK:(h + 1) * BLK].astype(F32)
        out[0, h] = total


def on_device(three_centre, occ_coeff, amp_coeff, col_blocks, slot_map, pair_list, pair_count):
    n_orb = lax.axis_size(ORB)
    n_far = lax.axis_size(FAR)
    own_rows, width = occ_coeff.shape
    half = own_rows // 2
    col_total = width // BLK

    aux, rows, sel = three_centre.shape
    vmem = pl.BlockSpec(memory_space=pltpu.VMEM)
    smem = pl.BlockSpec(memory_space=pltpu.SMEM)
    mine, g = pl.pallas_call(
        prepare_kernel,
        out_shape=(
            jax.ShapeDtypeStruct((n_orb, col_total * half, BLK), BF16),
            jax.ShapeDtypeStruct((aux * rows + TILE, sel), BF16),
        ),
        in_specs=[smem] * 3 + [vmem] * 3,
        out_specs=(vmem, vmem),
        name="prepare",
    )(pair_list, pair_count, slot_map, occ_coeff, amp_coeff, three_centre.reshape(aux * rows, sel))
    with jax.named_scope("g_side"):
        g_side = lax.ppermute(g, "zl", SWAP)
    with jax.named_scope("g_core"):
        g_core = lax.ppermute(g, "c", SWAP)
    with jax.named_scope("g_both"):
        g_both = lax.ppermute(g_side, "c", SWAP)
    got = lax.all_to_all(mine, ORB, 0, 0, tiled=True).reshape(n_orb, col_total, half, BLK)
    own = pl.pallas_call(
        select_kernel,
        out_shape=jax.ShapeDtypeStruct((NCB, n_orb, half, BLK), BF16),
        in_specs=[smem, vmem] + [pl.BlockSpec(memory_space=pl.ANY)] * 0,
        out_specs=vmem,
        compiler_params=pltpu.CompilerParams(vmem_limit_bytes=4 * 1024 * 1024),
        name="select_columns",
    )(col_blocks, got).reshape(NCB, n_orb * half, BLK)
    with jax.named_scope("other"):
        other = lax.ppermute(own, "yl", SWAP)
    near = jnp.stack((own, other), 0)
    with jax.named_scope("far"):
        far = lax.ppermute(near, "c", SWAP)
    coeffs = (near, far)
    slabs = (g, g_side, g_core, g_both)

    send = pl.pallas_call(
        exchange_kernel,
        out_shape=jax.ShapeDtypeStruct((n_far, OWN * BLK, BLK), BF16),
        in_specs=[vmem] * 4 + [pl.BlockSpec(memory_space=pl.ANY)] * 2,
        out_specs=vmem,
        scratch_shapes=[
            pltpu.VMEM((len(slabs), aux * rows, sel), BF16),
            pltpu.VMEM((2,) + g.shape, BF16),
            pltpu.VMEM((len(slabs), TILE, BLK), jnp.int32),
            pltpu.SMEM((len(slabs), TILE, BLK), jnp.int32),
            pltpu.SemaphoreType.DMA,
            pltpu.SemaphoreType.DMA((2,)),
        ],
        compiler_params=pltpu.CompilerParams(vmem_limit_bytes=12 * 1024 * 1024),
        name="exchange_blocks",
    )(*coeffs, *slabs)
    arrived = lax.all_to_all(send, FAR, 0, 0, tiled=True)
    return pl.pallas_call(
        sum_kernel,
        out_shape=jax.ShapeDtypeStruct((1, OWN, BLK, BLK), F32),
        in_specs=[vmem],
        out_specs=vmem,
        compiler_params=pltpu.CompilerParams(vmem_limit_bytes=12 * 1024 * 1024),
        name="sum_slots",
    )(arrived)


def solution(mesh):
    fine = Mesh(mesh.devices.reshape(8, 4, 2, 4, 2, 2), ("x", "yh", "yl", "zh", "zl", "c"))
    placed = (
        P(BAS, ORB, None),
        P(ORB, None),
        P(ORB, None),
        P(ORB, None),
        P(ORB, None),
        P(ORB, BAS, None),
        P(ORB, BAS),
    )
    return jax.shard_map(
        on_device,
        mesh=fine,
        in_specs=placed,
        out_specs=P(ORB, BAS, None, None),
        check_vma=False,
    )
```

```python
import jax
import jax.numpy as jnp
from jax import lax
from jax.experimental import pallas as pl
from jax.experimental.pallas import tpu as pltpu
from jax.sharding import Mesh, PartitionSpec as P

BLK = 128
NCB = 2
OWN = 2
AUX = 2
TILE = 16
ORB = ("x", "yh")
FAR = ("yl", "zh")
BAS = ("yl", "zh", "zl", "c")
SWAP = ((0, 1), (1, 0))
F32 = jnp.float32
BF16 = jnp.bfloat16


def contract(a, b, da, db):
    return lax.dot_general(a, b, (((da,), (db,)), ((), ())), preferred_element_type=F32)


def prepare_kernel(pairs, count, slots, occ, amp, g_ref, mine, packed):
    half = occ.shape[0] // 2
    tensor = jnp.where(lax.axis_index("yl") == 0, occ[...].astype(F32), amp[...].astype(F32))
    tensor = jnp.where(lax.axis_index("c") == 0, tensor[:half], tensor[half:])
    parts = [tensor[:, n * BLK:(n + 1) * BLK] for n in range(tensor.shape[1] // BLK)]
    block = jnp.concatenate(parts, axis=0).astype(BF16)
    for i in range(mine.shape[0]):
        mine[i] = block

    rows, width = g_ref.shape
    packed[0:rows] = g_ref[...]
    lane = lax.broadcasted_iota(jnp.int32, (TILE, width), 1)
    listed = jnp.full((TILE, width), -1, jnp.int32)
    for e in range(pairs.shape[2]):
        p = pairs[0, 0, e]
        here = jnp.where(e < count[0, 0], slots[0, p], -1)
        listed = jnp.where(lane == here, p, listed)
    packed[rows:rows + TILE] = listed.astype(F32).astype(BF16)


def exchange_kernel(*refs):
    coeffs, slabs = refs[0:4], refs[4:8]
    out, t_ref, held, wide_list, listed, sem, held_sem = refs[8:]
    fetches = [pltpu.make_async_copy(slabs[2 + i], held.at[i], held_sem.at[i]) for i in range(2)]
    for fetch in fetches:
        fetch.start()
    slabs = [slabs[0], slabs[1], held.at[0], held.at[1]]
    rows, width = t_ref.shape[1:]
    aux_blocks = rows // BLK
    row_blocks = aux_blocks // AUX

    def wide(parts):
        return jnp.concatenate(
            [jnp.concatenate([ref[k] for k in range(NCB)], axis=1) for ref in parts], axis=0
        )

    first, second = wide(coeffs[0:2]), wide(coeffs[2:4])
    is_occ = lax.axis_index("yl") == 0
    s = contract(jnp.where(is_occ, first, second), jnp.where(is_occ, second, first), 0, 0)
    s = s.astype(BF16)
    step = 2 * BLK
    for k, g_ref in enumerate(slabs):
        if k >= 2:
            fetches[k - 2].wait()
        wide_list[k] = g_ref[rows:rows + TILE, 0:BLK].astype(F32).astype(jnp.int32)
        if k == 3:
            copy = pltpu.make_async_copy(wide_list, listed, sem)
            copy.start()
        for m in range(0, rows, step):
            t_ref[k, m:m + step] = contract(g_ref[m:m + step], s, 1, 0).astype(BF16)
    copy.wait()

    quarter = lax.axis_index("zl") * 2 + lax.axis_index("c")

    def owner(j, _):
        slot = (j * 4 + quarter) * OWN
        total = [jnp.zeros((BLK, BLK), F32)] * OWN
        for k, g_ref in enumerate(slabs):
            pair = [listed[k, 0, slot + h] for h in range(OWN)]
            p = jnp.maximum(jnp.maximum(pair[0], pair[1]), 0)
            block = None
            for q in range(AUX):
                at = [
                    pl.ds(pl.multiple_of((q * row_blocks + r) * BLK, BLK), BLK)
                    for r in (p // row_blocks, p % row_blocks)
                ]
                term = contract(t_ref[k, at[0]], g_ref[at[1]], 1, 1)
                block = term if block is None else block + term
            total = [total[h] + jnp.where(pair[h] >= 0, block, 0.0) for h in range(OWN)]
        for h in range(OWN):
            out[j, h * BLK:(h + 1) * BLK] = total[h].astype(BF16)
        return 0

    lax.fori_loop(0, out.shape[0], owner, 0, unroll=True)


def select_kernel(columns, got, *rest):
    out = rest[-1]
    for k in range(NCB):
        out[k] = got[:, columns[0, k]]


def sum_kernel(got, out):
    for h in range(OWN):
        total = got[0, h * BLK:(h + 1) * BLK].astype(F32)
        for j in range(1, got.shape[0]):
            total = total + got[j, h * BLK:(h + 1) * BLK].astype(F32)
        out[0, h] = total


def on_device(three_centre, occ_coeff, amp_coeff, col_blocks, slot_map, pair_list, pair_count):
    n_orb = lax.axis_size(ORB)
    n_far = lax.axis_size(FAR)
    own_rows, width = occ_coeff.shape
    half = own_rows // 2
    col_total = width // BLK

    aux, rows, sel = three_centre.shape
    vmem = pl.BlockSpec(memory_space=pltpu.VMEM)
    smem = pl.BlockSpec(memory_space=pltpu.SMEM)
    mine, g = pl.pallas_call(
        prepare_kernel,
        out_shape=(
            jax.ShapeDtypeStruct((n_orb, col_total * half, BLK), BF16),
            jax.ShapeDtypeStruct((aux * rows + TILE, sel), BF16),
        ),
        in_specs=[smem] * 3 + [vmem] * 3,
        out_specs=(vmem, vmem),
        name="prepare",
    )(pair_list, pair_count, slot_map, occ_coeff, amp_coeff, three_centre.reshape(aux * rows, sel))
    with jax.named_scope("g_side"):
        g_side = lax.ppermute(g, "zl", SWAP)
    with jax.named_scope("g_core"):
        g_core = lax.ppermute(g, "c", SWAP)
    with jax.named_scope("g_both"):
        g_both = lax.ppermute(g_side, "c", SWAP)
    got = lax.all_to_all(mine, ORB, 0, 0, tiled=True).reshape(n_orb, col_total, half, BLK)
    own = pl.pallas_call(
        select_kernel,
        out_shape=jax.ShapeDtypeStruct((NCB, n_orb, half, BLK), BF16),
        in_specs=[smem, vmem] + [pl.BlockSpec(memory_space=pl.ANY)] * 0,
        out_specs=vmem,
        compiler_params=pltpu.CompilerParams(vmem_limit_bytes=4 * 1024 * 1024),
        name="select_columns",
    )(col_blocks, got).reshape(NCB, n_orb * half, BLK)
    with jax.named_scope("other"):
        other = lax.ppermute(own, "yl", SWAP)
    own_far = lax.ppermute(own, "c", SWAP)
    coeffs = (own, own_far, other, lax.ppermute(other, "c", SWAP))
    slabs = (g, g_side, g_core, g_both)

    send = pl.pallas_call(
        exchange_kernel,
        out_shape=jax.ShapeDtypeStruct((n_far, OWN * BLK, BLK), BF16),
        in_specs=[vmem] * (len(coeffs) + 2) + [pl.BlockSpec(memory_space=pl.ANY)] * 2,
        out_specs=vmem,
        scratch_shapes=[
            pltpu.VMEM((len(slabs), aux * rows, sel), BF16),
            pltpu.VMEM((2,) + g.shape, BF16),
            pltpu.VMEM((len(slabs), TILE, BLK), jnp.int32),
            pltpu.SMEM((len(slabs), TILE, BLK), jnp.int32),
            pltpu.SemaphoreType.DMA,
            pltpu.SemaphoreType.DMA((2,)),
        ],
        compiler_params=pltpu.CompilerParams(vmem_limit_bytes=12 * 1024 * 1024),
        name="exchange_blocks",
    )(*coeffs, *slabs)
    arrived = lax.all_to_all(send, FAR, 0, 0, tiled=True)
    return pl.pallas_call(
        sum_kernel,
        out_shape=jax.ShapeDtypeStruct((1, OWN, BLK, BLK), F32),
        in_specs=[vmem],
        out_specs=vmem,
        compiler_params=pltpu.CompilerParams(vmem_limit_bytes=12 * 1024 * 1024),
        name="sum_slots",
    )(arrived)


def solution(mesh):
    fine = Mesh(mesh.devices.reshape(8, 4, 2, 4, 2, 2), ("x", "yh", "yl", "zh", "zl", "c"))
    placed = (
        P(BAS, ORB, None),
        P(ORB, None),
        P(ORB, None),
        P(ORB, None),
        P(ORB, None),
        P(ORB, BAS, None),
        P(ORB, BAS),
    )
    return jax.shard_map(
        on_device,
        mesh=fine,
        in_specs=placed,
        out_specs=P(ORB, BAS, None, None),
        check_vma=False,
    )
```

```python
import jax
import jax.numpy as jnp
from jax import lax
from jax.experimental import pallas as pl
from jax.experimental.pallas import tpu as pltpu
from jax.sharding import Mesh, PartitionSpec as P

BLK = 128
NCB = 2
OWN = 2
AUX = 2
TILE = 16
ORB = ("x", "yh")
FAR = ("yl", "zh")
BAS = ("yl", "zh", "zl", "c")
SWAP = ((0, 1), (1, 0))
F32 = jnp.float32
BF16 = jnp.bfloat16


def contract(a, b, da, db):
    return lax.dot_general(a, b, (((da,), (db,)), ((), ())), preferred_element_type=F32)


def prepare_kernel(pairs, count, slots, occ, amp, g_ref, mine, packed):
    half = occ.shape[0] // 2
    tensor = jnp.where(lax.axis_index("yl") == 0, occ[...].astype(F32), amp[...].astype(F32))
    tensor = jnp.where(lax.axis_index("c") == 0, tensor[:half], tensor[half:])
    parts = [tensor[:, n * BLK:(n + 1) * BLK] for n in range(tensor.shape[1] // BLK)]
    block = jnp.concatenate(parts, axis=0).astype(BF16)
    for i in range(mine.shape[0]):
        mine[i] = block

    rows, width = g_ref.shape
    packed[0:rows] = g_ref[...]
    lane = lax.broadcasted_iota(jnp.int32, (8, BLK), 1)
    listed = jnp.full((8, BLK), -1, jnp.int32)
    for e in range(pairs.shape[2]):
        p = pairs[0, 0, e]
        here = jnp.where(e < count[0, 0], slots[0, p], -1)
        listed = jnp.where(lane == here, p, listed)
    listed = jnp.concatenate([listed.astype(F32)] * (TILE // 8), axis=0)
    packed[rows:rows + TILE] = jnp.concatenate([listed] * (width // BLK), axis=1).astype(BF16)


def exchange_kernel(*refs):
    coeffs, slabs = refs[0:4], refs[4:8]
    out, t_ref, held, wide_list, listed, sem, held_sem = refs[8:]
    fetches = [pltpu.make_async_copy(slabs[2 + i], held.at[i], held_sem.at[i]) for i in range(2)]
    for fetch in fetches:
        fetch.start()
    slabs = [slabs[0], slabs[1], held.at[0], held.at[1]]
    rows, width = t_ref.shape[1:]
    aux_blocks = rows // BLK
    row_blocks = aux_blocks // AUX

    def wide(parts):
        return jnp.concatenate(
            [jnp.concatenate([ref[k] for k in range(NCB)], axis=1) for ref in parts], axis=0
        )

    first, second = wide(coeffs[0:2]), wide(coeffs[2:4])
    is_occ = lax.axis_index("yl") == 0
    s = contract(jnp.where(is_occ, first, second), jnp.where(is_occ, second, first), 0, 0)
    s = s.astype(BF16)
    step = 2 * BLK
    for k, g_ref in enumerate(slabs):
        if k >= 2:
            fetches[k - 2].wait()
        wide_list[k] = g_ref[rows:rows + TILE, 0:BLK].astype(F32).astype(jnp.int32)
        if k == 3:
            copy = pltpu.make_async_copy(wide_list, listed, sem)
            copy.start()
        for m in range(0, rows, step):
            t_ref[k, m:m + step] = contract(g_ref[m:m + step], s, 1, 0).astype(BF16)
    copy.wait()

    quarter = lax.axis_index("zl") * 2 + lax.axis_index("c")

    def owner(j, _):
        slot = (j * 4 + quarter) * OWN
        total = [jnp.zeros((BLK, BLK), F32)] * OWN
        for k, g_ref in enumerate(slabs):
            pair = [listed[k, 0, slot + h] for h in range(OWN)]
            p = jnp.maximum(jnp.maximum(pair[0], pair[1]), 0)
            block = None
            for q in range(AUX):
                at = [
                    pl.ds(pl.multiple_of((q * row_blocks + r) * BLK, BLK), BLK)
                    for r in (p // row_blocks, p % row_blocks)
                ]
                term = contract(t_ref[k, at[0]], g_ref[at[1]], 1, 1)
                block = term if block is None else block + term
            total = [total[h] + jnp.where(pair[h] >= 0, block, 0.0) for h in range(OWN)]
        for h in range(OWN):
            out[j, h * BLK:(h + 1) * BLK] = total[h].astype(BF16)
        return 0

    lax.fori_loop(0, out.shape[0], owner, 0, unroll=True)


def select_kernel(columns, got, *rest):
    out = rest[-1]
    for k in range(NCB):
        out[k] = got[:, columns[0, k]]


def sum_kernel(got, out):
    for h in range(OWN):
        total = got[0, h * BLK:(h + 1) * BLK].astype(F32)
        for j in range(1, got.shape[0]):
            total = total + got[j, h * BLK:(h + 1) * BLK].astype(F32)
        out[0, h] = total


def on_device(three_centre, occ_coeff, amp_coeff, col_blocks, slot_map, pair_list, pair_count):
    n_orb = lax.axis_size(ORB)
    n_far = lax.axis_size(FAR)
    own_rows, width = occ_coeff.shape
    half = own_rows // 2
    col_total = width // BLK

    aux, rows, sel = three_centre.shape
    vmem = pl.BlockSpec(memory_space=pltpu.VMEM)
    smem = pl.BlockSpec(memory_space=pltpu.SMEM)
    mine, g = pl.pallas_call(
        prepare_kernel,
        out_shape=(
            jax.ShapeDtypeStruct((n_orb, col_total * half, BLK), BF16),
            jax.ShapeDtypeStruct((aux * rows + TILE, sel), BF16),
        ),
        in_specs=[smem] * 3 + [vmem] * 3,
        out_specs=(vmem, vmem),
        name="prepare",
    )(pair_list, pair_count, slot_map, occ_coeff, amp_coeff, three_centre.reshape(aux * rows, sel))
    with jax.named_scope("g_side"):
        g_side = lax.ppermute(g, "zl", SWAP)
    with jax.named_scope("g_core"):
        g_core = lax.ppermute(g, "c", SWAP)
    with jax.named_scope("g_both"):
        g_both = lax.ppermute(g_side, "c", SWAP)
    got = lax.all_to_all(mine, ORB, 0, 0, tiled=True).reshape(n_orb, col_total, half, BLK)
    own = pl.pallas_call(
        select_kernel,
        out_shape=jax.ShapeDtypeStruct((NCB, n_orb, half, BLK), BF16),
        in_specs=[smem, vmem] + [pl.BlockSpec(memory_space=pl.ANY)] * 0,
        out_specs=vmem,
        compiler_params=pltpu.CompilerParams(vmem_limit_bytes=4 * 1024 * 1024),
        name="select_columns",
    )(col_blocks, got).reshape(NCB, n_orb * half, BLK)
    with jax.named_scope("other"):
        other = lax.ppermute(own, "yl", SWAP)
    own_far = lax.ppermute(own, "c", SWAP)
    coeffs = (own, own_far, other, lax.ppermute(other, "c", SWAP))
    slabs = (g, g_side, g_core, g_both)

    send = pl.pallas_call(
        exchange_kernel,
        out_shape=jax.ShapeDtypeStruct((n_far, OWN * BLK, BLK), BF16),
        in_specs=[vmem] * (len(coeffs) + 2) + [pl.BlockSpec(memory_space=pl.ANY)] * 2,
        out_specs=vmem,
        scratch_shapes=[
            pltpu.VMEM((len(slabs), aux * rows, sel), BF16),
            pltpu.VMEM((2,) + g.shape, BF16),
            pltpu.VMEM((len(slabs), TILE, BLK), jnp.int32),
            pltpu.SMEM((len(slabs), TILE, BLK), jnp.int32),
            pltpu.SemaphoreType.DMA,
            pltpu.SemaphoreType.DMA((2,)),
        ],
        compiler_params=pltpu.CompilerParams(vmem_limit_bytes=12 * 1024 * 1024),
        name="exchange_blocks",
    )(*coeffs, *slabs)
    arrived = lax.all_to_all(send, FAR, 0, 0, tiled=True)
    return pl.pallas_call(
        sum_kernel,
        out_shape=jax.ShapeDtypeStruct((1, OWN, BLK, BLK), F32),
        in_specs=[vmem],
        out_specs=vmem,
        compiler_params=pltpu.CompilerParams(vmem_limit_bytes=12 * 1024 * 1024),
        name="sum_slots",
    )(arrived)


def solution(mesh):
    fine = Mesh(mesh.devices.reshape(8, 4, 2, 4, 2, 2), ("x", "yh", "yl", "zh", "zl", "c"))
    placed = (
        P(BAS, ORB, None),
        P(ORB, None),
        P(ORB, None),
        P(ORB, None),
        P(ORB, None),
        P(ORB, BAS, None),
        P(ORB, BAS),
    )
    return jax.shard_map(
        on_device,
        mesh=fine,
        in_specs=placed,
        out_specs=P(ORB, BAS, None, None),
        check_vma=False,
    )
```
